1024 devices in a mesh: grp: 16 (over x, y_lo, core), blk: 64 (over y_hi, z).
Axes of the slice: x: 4, y: 4 (y_hi: 2, y_lo: 2; y = y_hi * 2 + y_lo), z: 32, core: 2. Of those that a mesh axis runs over, the one named last changes fastest.
Arguments:
- picture_embeds: bfloat16 [131072, 1152], P(('grp', 'blk')), may hold values from -1 to 1
- caption_embeds: bfloat16 [131072, 1152], P(('grp', 'blk')), may hold values from -1 to 1
- holder_position: int32 [131072], P(('grp', 'blk')), may hold values from 0 to 63, as said below
- score_scaling: float32 [1], replicated, may hold values from 2 to 5
- score_offset_term: float32 [1], replicated, may hold values from -3 to 0
Outputs:
- image_grad: bfloat16 [131072, 1152], P(('grp', 'blk'))
- text_grad: bfloat16 [131072, 1152], P(('grp', 'blk'))
The draws below stay inside these ranges and needn't reach their ends.
Inputs may be any that keep to these rules, and one draw needn't show every extreme that they name: `holder_position`: of the 128 rows of one device at most 4 name any one position; in each group some position is named by exactly 4 rows of every device of the group.
All inputs are finite; a program needn't handle non-finite values.
Results may differ from the reference program's by a relative error of at most 0.005.
Values may be sent and summed in bfloat16 or wider, within the bound.
No kernel may reach another device: no remote copies, remote signals or barrier semaphores. Data moves between devices by JAX's collectives and lax.ppermute only.
A program may use at most 32 MiB of HBM per device.

```python
import jax
import jax.numpy as jnp
from jax import lax

D = 1152
ROWS_DEV = 128
STEPS = 2
CAP = 4
ROWS = 131072
N_GRP = 16
N_BLK = 64


def draw_holder_position(key, part):
    key = jax.random.fold_in(key, 11)
    blocks = N_GRP * N_BLK
    hot_pos = jax.random.randint(jax.random.fold_in(key, 1), (N_GRP,), 0, N_BLK)
    others = (N_BLK - 1) * CAP

    def one_block(index):
        block_key = jax.random.fold_in(key, 100 + index)
        first_key = jax.random.fold_in(block_key, 1)
        second_key = jax.random.fold_in(block_key, 2)
        popular_rows_present = hot_pos[index // N_BLK]
        pool = jnp.arange(others, dtype=jnp.int32) // CAP
        pool = jax.random.permutation(first_key, pool)[:ROWS_DEV - CAP]
        dispersion_factor = (popular_rows_present + 1 + pool) % N_BLK
        row_dest = jnp.concatenate([jnp.full((CAP,), popular_rows_present, jnp.int32), dispersion_factor.astype(jnp.int32)])
        return jax.random.permutation(second_key, row_dest)
    table = jax.vmap(one_block)(jnp.arange(blocks, dtype=jnp.int32))
    return table.reshape(ROWS_DEV * blocks).astype(jnp.int32)


def block_scale(stream_key, extent, split, smallest, top_value):
    gain = 1.0
    for position, shards_of in split:
        draws = jax.random.uniform(jax.random.fold_in(jax.random.fold_in(stream_key, 6), position), (shards_of,), jnp.float32, smallest / len(split), top_value / len(split))
        gain = gain * jnp.repeat(jnp.exp(draws), extent[position] // shards_of).reshape((-1,) + (1,) * (len(extent) - 1 - position))
    return gain


def scatter_about(rng, extent, scale, reach, pieces=(), kind=jnp.bfloat16):
    entries = jax.random.normal(rng, extent, jnp.float32) * scale
    if len(pieces) > 0:
        entries = block_scale(rng, extent, pieces, -0.22, 0.18) * entries
    return jnp.clip(entries, min=-reach, max=reach).astype(kind)


def setup_inputs(seed: int = 0) -> dict:
    streams_of = jax.random.split(jax.random.key(seed), 6)
    return {
        "picture_embeds": scatter_about(streams_of[0], (ROWS, D), 0.17, 1.0, ((0, 1024),)),
        "caption_embeds": scatter_about(streams_of[1], (ROWS, D), 0.17, 1.0, ((0, 1024),)),
        "holder_position": draw_holder_position(jax.random.fold_in(streams_of[5], 71), 0),
        "score_scaling": jnp.clip(jax.random.uniform(streams_of[3], (1,), jnp.float32, 2.0, 5.0), 2.0, 5.0),
        "score_offset_term": jnp.clip(jax.random.uniform(streams_of[4], (1,), jnp.float32, -3.0, 0.0), -3.0, 0.0),
    }


def weight_matrix(picture_batch, caption_batch, sharpness_multiplier, start_displacement, matching_label):
    pair_scores = sharpness_multiplier * jnp.dot(picture_batch, caption_batch.T, preferred_element_type=jnp.float32) + start_displacement
    return (sharpness_multiplier * (jax.nn.sigmoid(pair_scores) - matching_label)).astype(jnp.bfloat16)


def reference(picture_embeds, caption_embeds, holder_position, score_scaling, score_offset_term):
    devices = N_GRP * N_BLK
    slots = N_BLK * CAP
    sharpness_multiplier = score_scaling[0]
    start_displacement = score_offset_term[0]
    owner_block = holder_position.reshape(devices, ROWS_DEV).astype(jnp.int32)
    dest_hit = (owner_block[:, :, None] == jnp.arange(N_BLK, dtype=jnp.int32)[None, None, :]).astype(jnp.int32)
    rank_in = jnp.sum(jnp.cumsum(dest_hit, axis=1) * dest_hit, axis=2) - 1
    source_pos = (jnp.arange(devices, dtype=jnp.int32) % N_BLK)[:, None]
    slot_lookup = (source_pos * CAP + rank_in).reshape(-1).astype(jnp.int32)
    group_of = (jnp.arange(ROWS, dtype=jnp.int32) // (ROWS_DEV * N_BLK)).astype(jnp.int32)
    new_device = (group_of * N_BLK + holder_position.astype(jnp.int32)).astype(jnp.int32)
    where = (new_device * slots + slot_lookup).astype(jnp.int32)
    image_all = jnp.zeros((devices * slots, D), jnp.bfloat16).at[where].set(picture_embeds).reshape(devices, slots, D)
    text_all = jnp.zeros((devices * slots, D), jnp.bfloat16).at[where].set(caption_embeds).reshape(devices, slots, D)
    identity_square = jnp.eye(slots, dtype=jnp.float32)

    def image_side(worker_rank):
        picture_batch = image_all[worker_rank]
        total = jnp.zeros((slots, D), jnp.float32)
        for step in range(STEPS + 1):
            caption_batch = text_all[(worker_rank - step) % devices]
            matching_label = identity_square if step == 0 else jnp.float32(0.0)
            weight_entry = weight_matrix(picture_batch, caption_batch, sharpness_multiplier, start_displacement, matching_label)
            total = total + jnp.dot(weight_entry, caption_batch, preferred_element_type=jnp.float32)
        return total.astype(jnp.bfloat16)

    def text_side(worker_rank):
        caption_batch = text_all[worker_rank]
        total = jnp.zeros((slots, D), jnp.float32)
        for step in range(STEPS + 1):
            picture_batch = image_all[(worker_rank + step) % devices]
            matching_label = identity_square if step == 0 else jnp.float32(0.0)
            weight_entry = weight_matrix(picture_batch, caption_batch, sharpness_multiplier, start_displacement, matching_label)
            total = total + jnp.dot(weight_entry.T, picture_batch, preferred_element_type=jnp.float32)
        return total.astype(jnp.bfloat16)

    indices = jnp.arange(devices, dtype=jnp.int32)
    image_total = lax.map(image_side, indices).reshape(devices * slots, D)
    text_total = lax.map(text_side, indices).reshape(devices * slots, D)
    return image_total[where], text_total[where]
```

```python
import jax
import jax.numpy as jnp
from jax import lax
from jax.sharding import PartitionSpec as P

STEPS = 2
RING = ("grp", "blk")


def shifted(x, by):
    devices = lax.axis_size(RING)
    return lax.ppermute(x, RING, [(i, (i + by) % devices) for i in range(devices)])


def weight_matrix(picture_batch, caption_batch, scale, offset, matching_label):
    scores = lax.dot_general(
        picture_batch,
        caption_batch,
        (((1,), (1,)), ((), ())),
        preferred_element_type=jnp.float32,
    )
    pair_scores = scale * scores + offset
    return (scale * (jax.nn.sigmoid(pair_scores) - matching_label)).astype(jnp.bfloat16)


def times_rows(weights, rows):
    return jnp.dot(weights, rows, preferred_element_type=jnp.float32)


def rows_of_transpose(weights, rows):
    return lax.dot_general(
        weights, rows, (((0,), (0,)), ((), ())), preferred_element_type=jnp.float32
    )


def swap_blocks(x, blk_count):
    slots, width = x.shape
    out = lax.all_to_all(
        x.reshape(blk_count, slots // blk_count, width),
        "blk",
        split_axis=0,
        concat_axis=0,
        tiled=True,
    )
    return out.reshape(slots, width)


def body(picture_embeds, caption_embeds, holder_position, score_scaling, score_offset_term):
    rows_here, width = picture_embeds.shape
    blk_count = lax.axis_size("blk")
    capacity = 2 * rows_here // blk_count
    slots = blk_count * capacity
    scale = score_scaling[0]
    offset = score_offset_term[0]
    same = holder_position[:, None] == holder_position[None, :]
    order = jnp.arange(rows_here, dtype=jnp.int32)
    rank_in = jnp.sum((same & (order[None, :] < order[:, None])).astype(jnp.int32), axis=1)
    slot_lookup = holder_position * capacity + rank_in
    placer = (jnp.arange(slots, dtype=jnp.int32)[:, None] == slot_lookup[None, :]).astype(
        jnp.bfloat16
    )
    both = jnp.concatenate([picture_embeds, caption_embeds], axis=1)
    sent = times_rows(placer, both).astype(jnp.bfloat16)
    received = swap_blocks(sent, blk_count)
    pictures = received[:, :width]
    captions = received[:, width:]

    earlier_captions = [captions]
    later_pictures = [pictures]
    for _ in range(STEPS):
        earlier_captions.append(shifted(earlier_captions[-1], 1))
        later_pictures.append(shifted(later_pictures[-1], -1))

    identity_square = jnp.eye(slots, dtype=jnp.float32)
    own_weights = weight_matrix(pictures, captions, scale, offset, identity_square)
    image_total = times_rows(own_weights, captions)
    text_total = rows_of_transpose(own_weights, pictures)
    zero = jnp.float32(0.0)
    for step in range(1, STEPS + 1):
        weights = weight_matrix(pictures, earlier_captions[step], scale, offset, zero)
        image_total = image_total + times_rows(weights, earlier_captions[step])
        weights = weight_matrix(later_pictures[step], captions, scale, offset, zero)
        text_total = text_total + rows_of_transpose(weights, later_pictures[step])

    done = jnp.concatenate([image_total, text_total], axis=1).astype(jnp.bfloat16)
    back = swap_blocks(done, blk_count)
    grads = rows_of_transpose(placer, back).astype(jnp.bfloat16)
    return (grads[:, :width], grads[:, width:])


def solution(mesh):
    placed = (P(RING, None), P(RING, None), P(RING), P(), P())
    return jax.shard_map(
        body,
        mesh=mesh,
        in_specs=placed,
        out_specs=(P(RING, None), P(RING, None)),
        check_vma=False,
    )
```

```python
import jax
import jax.numpy as jnp
from jax import lax
from jax.sharding import Mesh, PartitionSpec as P

STEPS = 2
GRP, Y_HI, Z = 16, 2, 32
AXES = ("grp", "y_hi", "z_hi", "z_lo")
REGION = ("grp", "y_hi", "z_lo")


def device_at(x, y, core, z):
    return (((x * 2 + y % 2) * 2 + core) * Y_HI + y // 2) * Z + z


def routes():
    in_plane, along_z = [], []
    for g in range(GRP):
        for y_hi in range(Y_HI):
            for z in range(Z):
                column = (g - z + 8 * y_hi) % GRP
                source = (g * Y_HI + y_hi) * Z + z
                via = device_at(column // 4, column % 4, y_hi, z)
                held = device_at(column // 4, column % 4, y_hi, 2 * g + z // GRP)
                in_plane.append((source, via))
                along_z.append((via, held))
    return in_plane, along_z


IN_PLANE, ALONG_Z = routes()
VIA_TO_HELD = dict(ALONG_Z)
TO_REGION = [(source, VIA_TO_HELD[via]) for source, via in IN_PLANE]
FROM_REGION = [(held, source) for source, held in TO_REGION]


def owner_place(position):
    core, chip = position & 1, position >> 1
    x = (chip >> 2) & 3
    y = (chip - x) & 3
    return x, y, core, chip >> 4


def owner_device(owner):
    group, position = owner // 64, owner % 64
    x, y, core, z_lo = owner_place(position)
    return device_at(x, y, core, 2 * group + z_lo)


OWNERS = [owner_device(owner) for owner in range(GRP * Y_HI * Z)]
NEXT = [(OWNERS[i], OWNERS[(i + 1) % len(OWNERS)]) for i in range(len(OWNERS))]
BEFORE = [(b, a) for a, b in NEXT]


def moved(x, route):
    return lax.ppermute(x, AXES, route)


def weight_matrix(picture_batch, caption_batch, scale, offset, matching_label):
    scores = lax.dot_general(
        picture_batch,
        caption_batch,
        (((1,), (1,)), ((), ())),
        preferred_element_type=jnp.float32,
    )
    pair_scores = scale * scores + offset
    return (scale * (jax.nn.sigmoid(pair_scores) - matching_label)).astype(jnp.bfloat16)


def times_rows(weights, rows):
    return jnp.dot(weights, rows, preferred_element_type=jnp.float32)


def rows_of_transpose(weights, rows):
    return lax.dot_general(
        weights, rows, (((0,), (0,)), ((), ())), preferred_element_type=jnp.float32
    )


def swap_blocks(x, devices):
    slots, width = x.shape
    out = lax.all_to_all(
        x.reshape(devices, slots // devices, width),
        REGION,
        split_axis=0,
        concat_axis=0,
        tiled=True,
    )
    return out.reshape(slots, width)


def body(picture_embeds, caption_embeds, holder_position, score_scaling, score_offset_term):
    rows_here = picture_embeds.shape[0]
    devices = lax.axis_size(REGION)
    capacity = 2 * rows_here // devices
    slots = devices * capacity
    scale = score_scaling[0]
    offset = score_offset_term[0]

    position = moved(holder_position, TO_REGION)
    captions_via = moved(caption_embeds, IN_PLANE)
    pictures_via = moved(picture_embeds, IN_PLANE)
    captions_held = moved(captions_via, ALONG_Z)
    pictures_held = moved(pictures_via, ALONG_Z)

    same = position[:, None] == position[None, :]
    order = jnp.arange(rows_here, dtype=jnp.int32)
    rank_in = jnp.sum((same & (order[None, :] < order[:, None])).astype(jnp.int32), axis=1)
    x, y, core, z_lo = owner_place(position)
    owner = (((x * 2 + (y & 1)) * 2 + core) * 2 + (y >> 1)) * 2 + z_lo
    placer = (
        jnp.arange(slots, dtype=jnp.int32)[:, None] == (owner * capacity + rank_in)[None, :]
    ).astype(jnp.bfloat16)

    captions = swap_blocks(times_rows(placer, captions_held).astype(jnp.bfloat16), devices)
    pictures = swap_blocks(times_rows(placer, pictures_held).astype(jnp.bfloat16), devices)

    earlier_captions = [captions]
    later_pictures = [pictures]
    for _ in range(STEPS):
        earlier_captions.append(moved(earlier_captions[-1], NEXT))
        later_pictures.append(moved(later_pictures[-1], BEFORE))

    identity_square = jnp.eye(slots, dtype=jnp.float32)
    own_weights = weight_matrix(pictures, captions, scale, offset, identity_square)
    image_total = times_rows(own_weights, captions)
    text_total = rows_of_transpose(own_weights, pictures)
    zero = jnp.float32(0.0)
    for step in range(1, STEPS + 1):
        weights = weight_matrix(pictures, earlier_captions[step], scale, offset, zero)
        image_total = image_total + times_rows(weights, earlier_captions[step])
    image_back = swap_blocks(image_total.astype(jnp.bfloat16), devices)
    for step in range(1, STEPS + 1):
        weights = weight_matrix(later_pictures[step], captions, scale, offset, zero)
        text_total = text_total + rows_of_transpose(weights, later_pictures[step])
    text_back = swap_blocks(text_total.astype(jnp.bfloat16), devices)

    image_grad = moved(rows_of_transpose(placer, image_back).astype(jnp.bfloat16), FROM_REGION)
    text_grad = moved(rows_of_transpose(placer, text_back).astype(jnp.bfloat16), FROM_REGION)
    return (image_grad, text_grad)


def solution(mesh):
    cut = Mesh(mesh.devices.reshape(GRP, Y_HI, Z // 2, 2), AXES)
    placed = (P(AXES, None), P(AXES, None), P(AXES), P(), P())
    return jax.shard_map(
        body,
        mesh=cut,
        in_specs=placed,
        out_specs=(P(AXES, None), P(AXES, None)),
        check_vma=False,
    )
```

```python
import jax
import jax.numpy as jnp
from jax import lax
from jax.sharding import Mesh, PartitionSpec as P

STEPS = 2
GRP, Y_HI, Z = 16, 2, 32
AXES = ("grp", "y_hi", "z_hi", "z_lo")
REGION = ("grp", "y_hi", "z_lo")


def device_at(x, y, core, z):
    return (((x * 2 + y % 2) * 2 + core) * Y_HI + y // 2) * Z + z


def routes():
    in_plane, along_z = [], []
    for g in range(GRP):
        for y_hi in range(Y_HI):
            for z in range(Z):
                column = (3 * g - 3 * z + 8 * y_hi) % GRP
                source = (g * Y_HI + y_hi) * Z + z
                via = device_at(column // 4, column % 4, y_hi, z)
                held = device_at(column // 4, column % 4, y_hi, 2 * g + z // GRP)
                in_plane.append((source, via))
                along_z.append((via, held))
    return in_plane, along_z


IN_PLANE, ALONG_Z = routes()
VIA_TO_HELD = dict(ALONG_Z)
TO_REGION = [(source, VIA_TO_HELD[via]) for source, via in IN_PLANE]
FROM_REGION = [(held, source) for source, held in TO_REGION]


def owner_place(position):
    core, chip = position & 1, position >> 1
    x = (chip >> 2) & 3
    y = (chip - x) & 3
    return x, y, core, chip >> 4


def owner_device(owner):
    group, position = owner // 64, owner % 64
    x, y, core, z_lo = owner_place(position)
    return device_at(x, y, core, 2 * group + z_lo)


OWNERS = [owner_device(owner) for owner in range(GRP * Y_HI * Z)]
NEXT = [(OWNERS[i], OWNERS[(i + 1) % len(OWNERS)]) for i in range(len(OWNERS))]
BEFORE = [(b, a) for a, b in NEXT]


def moved(x, route):
    return lax.ppermute(x, AXES, route)


def weight_matrix(picture_batch, caption_batch, scale, offset, matching_label):
    scores = lax.dot_general(
        picture_batch,
        caption_batch,
        (((1,), (1,)), ((), ())),
        preferred_element_type=jnp.float32,
    )
    pair_scores = scale * scores + offset
    return (scale * (jax.nn.sigmoid(pair_scores) - matching_label)).astype(jnp.bfloat16)


def times_rows(weights, rows):
    return jnp.dot(weights, rows, preferred_element_type=jnp.float32)


def rows_of_transpose(weights, rows):
    return lax.dot_general(
        weights, rows, (((0,), (0,)), ((), ())), preferred_element_type=jnp.float32
    )


def swap_blocks(x, devices):
    slots, width = x.shape
    out = lax.all_to_all(
        x.reshape(devices, slots // devices, width),
        REGION,
        split_axis=0,
        concat_axis=0,
        tiled=True,
    )
    return out.reshape(slots, width)


def body(picture_embeds, caption_embeds, holder_position, score_scaling, score_offset_term):
    rows_here, width = picture_embeds.shape
    devices = lax.axis_size(REGION)
    capacity = 2 * rows_here // devices
    slots = devices * capacity
    scale = score_scaling[0]
    offset = score_offset_term[0]

    position = moved(holder_position, TO_REGION)
    captions_via = moved(caption_embeds, IN_PLANE)
    captions_via, picture_embeds, position = lax.optimization_barrier(
        (captions_via, picture_embeds, position)
    )
    pictures_via = moved(picture_embeds, IN_PLANE)
    captions_held = moved(captions_via, ALONG_Z)
    pictures_held = moved(pictures_via, ALONG_Z)

    same = position[:, None] == position[None, :]
    order = jnp.arange(rows_here, dtype=jnp.int32)
    rank_in = jnp.sum((same & (order[None, :] < order[:, None])).astype(jnp.int32), axis=1)
    x, y, core, z_lo = owner_place(position)
    owner = (((x * 2 + (y & 1)) * 2 + core) * 2 + (y >> 1)) * 2 + z_lo
    placer = (
        jnp.arange(slots, dtype=jnp.int32)[:, None] == (owner * capacity + rank_in)[None, :]
    ).astype(jnp.bfloat16)

    placed = [times_rows(placer, held) for held in (pictures_held, captions_held)]
    received = swap_blocks(jnp.concatenate(placed, axis=1).astype(jnp.bfloat16), devices)
    pictures = received[:, :width]
    captions = received[:, width:]

    earlier_captions = [captions]
    later_pictures = [pictures]
    for _ in range(STEPS):
        earlier_captions.append(moved(earlier_captions[-1], NEXT))
        later_pictures.append(moved(later_pictures[-1], BEFORE))

    identity_square = jnp.eye(slots, dtype=jnp.float32)
    own_weights = weight_matrix(pictures, captions, scale, offset, identity_square)
    image_total = times_rows(own_weights, captions)
    text_total = rows_of_transpose(own_weights, pictures)
    zero = jnp.float32(0.0)
    for step in range(1, STEPS + 1):
        weights = weight_matrix(pictures, earlier_captions[step], scale, offset, zero)
        image_total = image_total + times_rows(weights, earlier_captions[step])
    image_done = image_total.astype(jnp.bfloat16)
    image_done, *later_pictures = lax.optimization_barrier((image_done, *later_pictures))
    image_back = swap_blocks(image_done, devices)
    image_grad = moved(rows_of_transpose(placer, image_back).astype(jnp.bfloat16), FROM_REGION)

    for step in range(1, STEPS + 1):
        weights = weight_matrix(later_pictures[step], captions, scale, offset, zero)
        text_total = text_total + rows_of_transpose(weights, later_pictures[step])
    text_back = swap_blocks(text_total.astype(jnp.bfloat16), devices)
    text_grad = moved(rows_of_transpose(placer, text_back).astype(jnp.bfloat16), FROM_REGION)
    return (image_grad, text_grad)


def solution(mesh):
    cut = Mesh(mesh.devices.reshape(GRP, Y_HI, Z // 2, 2), AXES)
    placed = (P(AXES, None), P(AXES, None), P(AXES), P(), P())
    return jax.shard_map(
        body,
        mesh=cut,
        in_specs=placed,
        out_specs=(P(AXES, None), P(AXES, None)),
        check_vma=False,
    )
```

```python
import jax
import jax.numpy as jnp
from jax import lax
from jax.sharding import Mesh, PartitionSpec as P

STEPS = 2
GRP, Y_HI, Z = 16, 2, 32
AXES = ("grp", "y_hi", "z_hi", "z_lo")
REGION = ("grp", "y_hi", "z_lo")


def device_at(x, y, core, z):
    return (((x * 2 + y % 2) * 2 + core) * Y_HI + y // 2) * Z + z


def routes():
    in_plane, along_z = [], []
    for g in range(GRP):
        for y_hi in range(Y_HI):
            for z in range(Z):
                column = (3 * g + z + 8 * y_hi) % GRP
                z_lo = (2 * g - z) % Z // GRP
                source = (g * Y_HI + y_hi) * Z + z
                via = device_at(column // 4, column % 4, y_hi, z)
                held = device_at(column // 4, column % 4, y_hi, 2 * g + z_lo)
                in_plane.append((source, via))
                along_z.append((via, held))
    return in_plane, along_z


IN_PLANE, ALONG_Z = routes()
VIA_TO_HELD = dict(ALONG_Z)
TO_REGION = [(source, VIA_TO_HELD[via]) for source, via in IN_PLANE]
FROM_REGION = [(held, source) for source, held in TO_REGION]


def owner_place(position):
    core, chip = position & 1, position >> 1
    x = (chip >> 2) & 3
    y = (chip - x) & 3
    return x, y, core, chip >> 4


def owner_device(owner):
    group, position = owner // 64, owner % 64
    x, y, core, z_lo = owner_place(position)
    return device_at(x, y, core, 2 * group + z_lo)


OWNERS = [owner_device(owner) for owner in range(GRP * Y_HI * Z)]
NEXT = [(OWNERS[i], OWNERS[(i + 1) % len(OWNERS)]) for i in range(len(OWNERS))]
BEFORE = [(b, a) for a, b in NEXT]


def moved(x, route):
    return lax.ppermute(x, AXES, route)


def weight_matrix(picture_batch, caption_batch, scale, offset, matching_label):
    scores = lax.dot_general(
        picture_batch,
        caption_batch,
        (((1,), (1,)), ((), ())),
        preferred_element_type=jnp.float32,
    )
    pair_scores = scale * scores + offset
    return (scale * (jax.nn.sigmoid(pair_scores) - matching_label)).astype(jnp.bfloat16)


def times_rows(weights, rows):
    return jnp.dot(weights, rows, preferred_element_type=jnp.float32)


def rows_of_transpose(weights, rows):
    return lax.dot_general(
        weights, rows, (((0,), (0,)), ((), ())), preferred_element_type=jnp.float32
    )


def swap_blocks(x, devices):
    slots, width = x.shape
    out = lax.all_to_all(
        x.reshape(devices, slots // devices, width),
        REGION,
        split_axis=0,
        concat_axis=0,
        tiled=True,
    )
    return out.reshape(slots, width)


def body(picture_embeds, caption_embeds, holder_position, score_scaling, score_offset_term):
    rows_here, width = picture_embeds.shape
    devices = lax.axis_size(REGION)
    capacity = 2 * rows_here // devices
    slots = devices * capacity
    scale = score_scaling[0]
    offset = score_offset_term[0]

    position = moved(holder_position, TO_REGION)
    both = jnp.concatenate([picture_embeds, caption_embeds], axis=1)
    held = moved(moved(both, IN_PLANE), ALONG_Z)

    same = position[:, None] == position[None, :]
    order = jnp.arange(rows_here, dtype=jnp.int32)
    rank_in = jnp.sum((same & (order[None, :] < order[:, None])).astype(jnp.int32), axis=1)
    x, y, core, z_lo = owner_place(position)
    owner = (((x * 2 + (y & 1)) * 2 + core) * 2 + (y >> 1)) * 2 + z_lo
    placer = (
        jnp.arange(slots, dtype=jnp.int32)[:, None] == (owner * capacity + rank_in)[None, :]
    ).astype(jnp.bfloat16)

    received = swap_blocks(times_rows(placer, held).astype(jnp.bfloat16), devices)
    pictures = received[:, :width]
    captions = received[:, width:]

    earlier_captions = [captions]
    later_pictures = [pictures]
    for _ in range(STEPS):
        earlier_captions.append(moved(earlier_captions[-1], NEXT))
        later_pictures.append(moved(later_pictures[-1], BEFORE))

    identity_square = jnp.eye(slots, dtype=jnp.float32)
    own_weights = weight_matrix(pictures, captions, scale, offset, identity_square)
    image_total = times_rows(own_weights, captions)
    text_total = rows_of_transpose(own_weights, pictures)
    zero = jnp.float32(0.0)
    for step in range(1, STEPS + 1):
        weights = weight_matrix(pictures, earlier_captions[step], scale, offset, zero)
        image_total = image_total + times_rows(weights, earlier_captions[step])
        weights = weight_matrix(later_pictures[step], captions, scale, offset, zero)
        text_total = text_total + rows_of_transpose(weights, later_pictures[step])

    done = jnp.concatenate([image_total, text_total], axis=1).astype(jnp.bfloat16)
    back = swap_blocks(done, devices)
    grads = moved(rows_of_transpose(placer, back).astype(jnp.bfloat16), FROM_REGION)
    return (grads[:, :width], grads[:, width:])


def solution(mesh):
    cut = Mesh(mesh.devices.reshape(GRP, Y_HI, Z // 2, 2), AXES)
    placed = (P(AXES, None), P(AXES, None), P(AXES), P(), P())
    return jax.shard_map(
        body,
        mesh=cut,
        in_specs=placed,
        out_specs=(P(AXES, None), P(AXES, None)),
        check_vma=False,
    )
```

```python
import jax
import jax.numpy as jnp
from jax import lax
from jax.experimental import pallas as pl
from jax.experimental.pallas import tpu as pltpu
from jax.sharding import Mesh, PartitionSpec as P

STEPS = 2
GRP, Y_HI, Z = 16, 2, 32
AXES = ("grp", "y_hi", "z_hi", "z_lo")
REGION = ("grp", "y_hi", "z_lo")


def device_at(x, y, core, z):
    return (((x * 2 + y % 2) * 2 + core) * Y_HI + y // 2) * Z + z


def routes():
    in_plane, along_z = [], []
    for g in range(GRP):
        for y_hi in range(Y_HI):
            for z in range(Z):
                column = (3 * g + z + 8 * y_hi) % GRP
                z_lo = (2 * g - z) % Z // GRP
                source = (g * Y_HI + y_hi) * Z + z
                via = device_at(column // 4, column % 4, y_hi, z)
                held = device_at(column // 4, column % 4, y_hi, 2 * g + z_lo)
                in_plane.append((source, via))
                along_z.append((via, held))
    return in_plane, along_z


IN_PLANE, ALONG_Z = routes()
VIA_TO_HELD = dict(ALONG_Z)
TO_REGION = [(source, VIA_TO_HELD[via]) for source, via in IN_PLANE]
FROM_REGION = [(held, source) for source, held in TO_REGION]


def owner_place(position):
    core, chip = position & 1, position >> 1
    x = (chip >> 2) & 3
    y = (chip - x) & 3
    return x, y, core, chip >> 4


def owner_device(owner):
    group, position = owner // 64, owner % 64
    x, y, core, z_lo = owner_place(position)
    return device_at(x, y, core, 2 * group + z_lo)


OWNERS = [owner_device(owner) for owner in range(GRP * Y_HI * Z)]
NEXT = [(OWNERS[i], OWNERS[(i + 1) % len(OWNERS)]) for i in range(len(OWNERS))]
BEFORE = [(b, a) for a, b in NEXT]


def moved(x, route):
    return lax.ppermute(x, AXES, route)


TILE = 384


def gradients_kernel(scale_ref, offset_ref, p0, p1, p2, c0, c1, c2, out_ref):
    slots, width = p0.shape
    scale, offset = scale_ref[0], offset_ref[0]
    shape = (slots, slots)
    same = lax.broadcasted_iota(jnp.int32, shape, 0) == lax.broadcasted_iota(jnp.int32, shape, 1)
    identity_square = jnp.where(same, jnp.float32(1.0), jnp.float32(0.0))

    def weights(left, right, matching_label):
        scores = lax.dot_general(
            left[...], right[...], (((1,), (1,)), ((), ())), preferred_element_type=jnp.float32
        )
        coef = jax.nn.sigmoid(scale * scores + offset) - matching_label
        return (scale * coef).astype(jnp.bfloat16)

    zero = jnp.float32(0.0)
    for rows, others, start in ((p0, (c0, c1, c2), 0), (c0, (p0, p1, p2), width)):
        mixed = [
            weights(rows, other, identity_square if n == 0 else zero)
            for n, other in enumerate(others)
        ]
        for at in range(0, width, TILE):
            total = sum(
                jnp.dot(w, other[:, at : at + TILE], preferred_element_type=jnp.float32)
                for w, other in zip(mixed, others)
            )
            out_ref[:, start + at : start + at + TILE] = total.astype(out_ref.dtype)


def gradients(scale, offset, pictures, captions):
    slots, width = pictures[0].shape
    arrays = [*pictures, *captions]
    flops = 12 * 2 * slots * slots * width
    return pl.pallas_call(
        gradients_kernel,
        out_shape=jax.ShapeDtypeStruct((slots, 2 * width), jnp.bfloat16),
        in_specs=[pl.BlockSpec(memory_space=pltpu.SMEM)] * 2
        + [pl.BlockSpec(memory_space=pltpu.VMEM)] * len(arrays),
        out_specs=pl.BlockSpec(memory_space=pltpu.VMEM),
        compiler_params=pltpu.CompilerParams(vmem_limit_bytes=24 * 1024 * 1024),
        cost_estimate=pl.CostEstimate(
            flops=flops, bytes_accessed=16 * slots * width, transcendentals=6 * slots * slots
        ),
        name="gradients",
    )(scale, offset, *arrays)


def times_rows(weights, rows):
    return jnp.dot(weights, rows, preferred_element_type=jnp.float32)


def rows_of_transpose(weights, rows):
    return lax.dot_general(
        weights, rows, (((0,), (0,)), ((), ())), preferred_element_type=jnp.float32
    )


def swap_blocks(x, devices):
    slots, width = x.shape
    out = lax.all_to_all(
        x.reshape(devices, slots // devices, width),
        REGION,
        split_axis=0,
        concat_axis=0,
        tiled=True,
    )
    return out.reshape(slots, width)


def body(picture_embeds, caption_embeds, holder_position, score_scaling, score_offset_term):
    rows_here, width = picture_embeds.shape
    devices = lax.axis_size(REGION)
    capacity = 2 * rows_here // devices
    slots = devices * capacity

    position = moved(holder_position, TO_REGION)
    both = jnp.concatenate([picture_embeds, caption_embeds], axis=1)
    held = moved(moved(both, IN_PLANE), ALONG_Z)

    same = position[:, None] == position[None, :]
    order = jnp.arange(rows_here, dtype=jnp.int32)
    rank_in = jnp.sum((same & (order[None, :] < order[:, None])).astype(jnp.int32), axis=1)
    x, y, core, z_lo = owner_place(position)
    owner = (((x * 2 + (y & 1)) * 2 + core) * 2 + (y >> 1)) * 2 + z_lo
    placer = (
        jnp.arange(slots, dtype=jnp.int32)[:, None] == (owner * capacity + rank_in)[None, :]
    ).astype(jnp.bfloat16)

    received = swap_blocks(times_rows(placer, held).astype(jnp.bfloat16), devices)
    pictures = received[:, :width]
    captions = received[:, width:]

    earlier_captions = [captions]
    later_pictures = [pictures]
    for _ in range(STEPS):
        earlier_captions.append(moved(earlier_captions[-1], NEXT))
        later_pictures.append(moved(later_pictures[-1], BEFORE))

    done = gradients(score_scaling, score_offset_term, later_pictures, earlier_captions)
    back = swap_blocks(done, devices)
    grads = moved(rows_of_transpose(placer, back).astype(jnp.bfloat16), FROM_REGION)
    return (grads[:, :width], grads[:, width:])


def solution(mesh):
    cut = Mesh(mesh.devices.reshape(GRP, Y_HI, Z // 2, 2), AXES)
    placed = (P(AXES, None), P(AXES, None), P(AXES), P(), P())
    return jax.shard_map(
        body,
        mesh=cut,
        in_specs=placed,
        out_specs=(P(AXES, None), P(AXES, None)),
        check_vma=False,
    )
```

```python
import jax
import jax.numpy as jnp
from jax import lax
from jax.experimental import pallas as pl
from jax.experimental.pallas import tpu as pltpu
from jax.sharding import Mesh, PartitionSpec as P

STEPS = 2
GRP, Y_HI, Z = 16, 2, 32
AXES = ("grp", "y_hi", "z_hi", "z_lo")
REGION = ("grp", "y_hi", "z_lo")


def device_at(x, y, core, z):
    return (((x * 2 + y % 2) * 2 + core) * Y_HI + y // 2) * Z + z


def routes():
    in_plane, along_z = [], []
    for g in range(GRP):
        for y_hi in range(Y_HI):
            for z in range(Z):
                column = (3 * g + z + 8 * y_hi) % GRP
                z_lo = (2 * g - z) % Z // GRP
                source = (g * Y_HI + y_hi) * Z + z
                via = device_at(column // 4, column % 4, y_hi, z)
                held = device_at(column // 4, column % 4, y_hi, 2 * g + z_lo)
                in_plane.append((source, via))
                along_z.append((via, held))
    return in_plane, along_z


IN_PLANE, ALONG_Z = routes()
VIA_TO_HELD = dict(ALONG_Z)
TO_REGION = [(source, VIA_TO_HELD[via]) for source, via in IN_PLANE]
FROM_REGION = [(held, source) for source, held in TO_REGION]


def owner_place(position):
    core, chip = position & 1, position >> 1
    x = (chip >> 2) & 3
    y = (chip - x) & 3
    return x, y, core, chip >> 4


def owner_device(owner):
    group, position = owner // 64, owner % 64
    x, y, core, z_lo = owner_place(position)
    return device_at(x, y, core, 2 * group + z_lo)


OWNERS = [owner_device(owner) for owner in range(GRP * Y_HI * Z)]
NEXT = [(OWNERS[i], OWNERS[(i + 1) % len(OWNERS)]) for i in range(len(OWNERS))]
BEFORE = [(b, a) for a, b in NEXT]


def moved(x, route):
    return lax.ppermute(x, AXES, route)


TILE = 384


def gradients_kernel(scale_ref, offset_ref, p0, p1, p2, c0, c1, c2, out_ref):
    slots, width = p0.shape
    scale, offset = scale_ref[0], offset_ref[0]
    shape = (slots, slots)
    same = lax.broadcasted_iota(jnp.int32, shape, 0) == lax.broadcasted_iota(jnp.int32, shape, 1)
    identity_square = jnp.where(same, jnp.float32(1.0), jnp.float32(0.0))

    def weights(left, right, matching_label):
        scores = lax.dot_general(
            left[...], right[...], (((1,), (1,)), ((), ())), preferred_element_type=jnp.float32
        )
        coef = jax.nn.sigmoid(scale * scores + offset) - matching_label
        return (scale * coef).astype(jnp.bfloat16)

    zero = jnp.float32(0.0)
    for rows, others, start in ((p0, (c0, c1, c2), 0), (c0, (p0, p1, p2), width)):
        mixed = [
            weights(rows, other, identity_square if n == 0 else zero)
            for n, other in enumerate(others)
        ]
        for at in range(0, width, TILE):
            total = sum(
                jnp.dot(w, other[:, at : at + TILE], preferred_element_type=jnp.float32)
                for w, other in zip(mixed, others)
            )
            out_ref[:, start + at : start + at + TILE] = total.astype(out_ref.dtype)


def gradients(scale, offset, pictures, captions):
    slots, width = pictures[0].shape
    arrays = [*pictures, *captions]
    flops = 12 * 2 * slots * slots * width
    return pl.pallas_call(
        gradients_kernel,
        out_shape=jax.ShapeDtypeStruct((slots, 2 * width), jnp.bfloat16),
        in_specs=[pl.BlockSpec(memory_space=pltpu.SMEM)] * 2
        + [pl.BlockSpec(memory_space=pltpu.VMEM)] * len(arrays),
        out_specs=pl.BlockSpec(memory_space=pltpu.VMEM),
        compiler_params=pltpu.CompilerParams(vmem_limit_bytes=24 * 1024 * 1024),
        cost_estimate=pl.CostEstimate(
            flops=flops, bytes_accessed=16 * slots * width, transcendentals=6 * slots * slots
        ),
        name="gradients",
    )(scale, offset, *arrays)


def times_rows(weights, rows):
    return jnp.dot(weights, rows, preferred_element_type=jnp.float32)


def rows_of_transpose(weights, rows):
    return lax.dot_general(
        weights, rows, (((0,), (0,)), ((), ())), preferred_element_type=jnp.float32
    )


def swap_blocks(x, devices):
    slots, width = x.shape
    out = lax.all_to_all(
        x.reshape(devices, slots // devices, width),
        REGION,
        split_axis=0,
        concat_axis=0,
        tiled=True,
    )
    return out.reshape(slots, width)


def body(picture_embeds, caption_embeds, holder_position, score_scaling, score_offset_term):
    rows_here, width = picture_embeds.shape
    devices = lax.axis_size(REGION)
    capacity = 2 * rows_here // devices
    slots = devices * capacity

    position = moved(holder_position, TO_REGION)
    both = jnp.concatenate([picture_embeds, caption_embeds], axis=1)
    via, position = lax.optimization_barrier((moved(both, IN_PLANE), position))
    held = moved(via, ALONG_Z)

    same = position[:, None] == position[None, :]
    order = jnp.arange(rows_here, dtype=jnp.int32)
    rank_in = jnp.sum((same & (order[None, :] < order[:, None])).astype(jnp.int32), axis=1)
    x, y, core, z_lo = owner_place(position)
    owner = (((x * 2 + (y & 1)) * 2 + core) * 2 + (y >> 1)) * 2 + z_lo
    placer = (
        jnp.arange(slots, dtype=jnp.int32)[:, None] == (owner * capacity + rank_in)[None, :]
    ).astype(jnp.bfloat16)

    received = swap_blocks(times_rows(placer, held).astype(jnp.bfloat16), devices)
    pictures = received[:, :width]
    captions = received[:, width:]

    earlier_captions = [captions]
    later_pictures = [pictures]
    for _ in range(STEPS):
        earlier_captions.append(moved(earlier_captions[-1], NEXT))
        later_pictures.append(moved(later_pictures[-1], BEFORE))

    done = gradients(score_scaling, score_offset_term, later_pictures, earlier_captions)
    back = swap_blocks(done, devices)
    grads = moved(rows_of_transpose(placer, back).astype(jnp.bfloat16), FROM_REGION)
    return (grads[:, :width], grads[:, width:])


def solution(mesh):
    cut = Mesh(mesh.devices.reshape(GRP, Y_HI, Z // 2, 2), AXES)
    placed = (P(AXES, None), P(AXES, None), P(AXES), P(), P())
    return jax.shard_map(
        body,
        mesh=cut,
        in_specs=placed,
        out_specs=(P(AXES, None), P(AXES, None)),
        check_vma=False,
    )
```

```python
import jax
import jax.numpy as jnp
from jax import lax
from jax.experimental import pallas as pl
from jax.experimental.pallas import tpu as pltpu
from jax.sharding import Mesh, PartitionSpec as P

STEPS = 2
GRP, Y_HI, Z = 16, 2, 32
AXES = ("grp", "y_hi", "z_hi", "z_lo")
REGION = ("grp", "y_hi", "z_lo")


def device_at(x, y, core, z):
    return (((x * 2 + y % 2) * 2 + core) * Y_HI + y // 2) * Z + z


def routes():
    in_plane, along_z = [], []
    for g in range(GRP):
        for y_hi in range(Y_HI):
            for z in range(Z):
                column = (3 * g + z + 8 * y_hi) % GRP
                z_lo = (2 * g - z) % Z // GRP
                source = (g * Y_HI + y_hi) * Z + z
                via = device_at(column // 4, column % 4, y_hi, z)
                held = device_at(column // 4, column % 4, y_hi, 2 * g + z_lo)
                in_plane.append((source, via))
                along_z.append((via, held))
    return in_plane, along_z


IN_PLANE, ALONG_Z = routes()
VIA_TO_HELD = dict(ALONG_Z)
TO_REGION = [(source, VIA_TO_HELD[via]) for source, via in IN_PLANE]
FROM_REGION = [(held, source) for source, held in TO_REGION]


def owner_place(position):
    core, chip = position & 1, position >> 1
    x = (chip >> 2) & 3
    y = (chip - x) & 3
    return x, y, core, chip >> 4


def owner_device(owner):
    group, position = owner // 64, owner % 64
    x, y, core, z_lo = owner_place(position)
    return device_at(x, y, core, 2 * group + z_lo)


OWNERS = [owner_device(owner) for owner in range(GRP * Y_HI * Z)]


def owners_on(by):
    return [(OWNERS[i], OWNERS[(i + by) % len(OWNERS)]) for i in range(len(OWNERS))]


def moved(x, route):
    return lax.ppermute(x, AXES, route)


TILE = 384


def gradients_kernel(scale_ref, offset_ref, p0, c0, p1, c1, p2, c2, out_ref):
    slots, width = p0.shape
    scale, offset = scale_ref[0], offset_ref[0]
    shape = (slots, slots)
    same = lax.broadcasted_iota(jnp.int32, shape, 0) == lax.broadcasted_iota(jnp.int32, shape, 1)
    identity_square = jnp.where(same, jnp.float32(1.0), jnp.float32(0.0))

    def weights(left, right, matching_label):
        scores = lax.dot_general(
            left[...], right[...], (((1,), (1,)), ((), ())), preferred_element_type=jnp.float32
        )
        coef = jax.nn.sigmoid(scale * scores + offset) - matching_label
        return (scale * coef).astype(jnp.bfloat16)

    zero = jnp.float32(0.0)
    for rows, others, start in ((p0, (c0, c1, c2), 0), (c0, (p0, p1, p2), width)):
        mixed = [
            weights(rows, other, identity_square if n == 0 else zero)
            for n, other in enumerate(others)
        ]
        for at in range(0, width, TILE):
            total = sum(
                jnp.dot(w, other[:, at : at + TILE], preferred_element_type=jnp.float32)
                for w, other in zip(mixed, others)
            )
            out_ref[:, start + at : start + at + TILE] = total.astype(out_ref.dtype)


def gradients(scale, offset, pictures, captions):
    slots, width = pictures[0].shape
    arrays = [array for pair in zip(pictures, captions) for array in pair]
    flops = 12 * 2 * slots * slots * width
    return pl.pallas_call(
        gradients_kernel,
        out_shape=jax.ShapeDtypeStruct((slots, 2 * width), jnp.bfloat16),
        in_specs=[pl.BlockSpec(memory_space=pltpu.SMEM)] * 2
        + [pl.BlockSpec(memory_space=pltpu.VMEM)] * len(arrays),
        out_specs=pl.BlockSpec(memory_space=pltpu.VMEM),
        compiler_params=pltpu.CompilerParams(vmem_limit_bytes=24 * 1024 * 1024),
        cost_estimate=pl.CostEstimate(
            flops=flops, bytes_accessed=16 * slots * width, transcendentals=6 * slots * slots
        ),
        name="gradients",
    )(scale, offset, *arrays)


def times_rows(weights, rows):
    return jnp.dot(weights, rows, preferred_element_type=jnp.float32)


def rows_of_transpose(weights, rows):
    return lax.dot_general(
        weights, rows, (((0,), (0,)), ((), ())), preferred_element_type=jnp.float32
    )


def swap_blocks(x, devices):
    slots, width = x.shape
    out = lax.all_to_all(
        x.reshape(devices, slots // devices, width),
        REGION,
        split_axis=0,
        concat_axis=0,
        tiled=True,
    )
    return out.reshape(slots, width)


def body(picture_embeds, caption_embeds, holder_position, score_scaling, score_offset_term):
    rows_here, width = picture_embeds.shape
    devices = lax.axis_size(REGION)
    capacity = 2 * rows_here // devices
    slots = devices * capacity

    position = moved(holder_position, TO_REGION)
    both = jnp.concatenate([picture_embeds, caption_embeds], axis=1)
    held = moved(moved(both, IN_PLANE), ALONG_Z)

    same = position[:, None] == position[None, :]
    order = jnp.arange(rows_here, dtype=jnp.int32)
    rank_in = jnp.sum((same & (order[None, :] < order[:, None])).astype(jnp.int32), axis=1)
    x, y, core, z_lo = owner_place(position)
    owner = (((x * 2 + (y & 1)) * 2 + core) * 2 + (y >> 1)) * 2 + z_lo
    placer = (
        jnp.arange(slots, dtype=jnp.int32)[:, None] == (owner * capacity + rank_in)[None, :]
    ).astype(jnp.bfloat16)

    received = swap_blocks(times_rows(placer, held).astype(jnp.bfloat16), devices)
    pictures = received[:, :width]
    captions = received[:, width:]

    earlier_captions = [captions]
    later_pictures = [pictures]
    for step in range(1, STEPS + 1):
        later_pictures.append(moved(pictures, owners_on(-step)))
        earlier_captions.append(moved(captions, owners_on(step)))

    done = gradients(score_scaling, score_offset_term, later_pictures, earlier_captions)
    back = swap_blocks(done, devices)
    grads = moved(rows_of_transpose(placer, back).astype(jnp.bfloat16), FROM_REGION)
    return (grads[:, :width], grads[:, width:])


def solution(mesh):
    cut = Mesh(mesh.devices.reshape(GRP, Y_HI, Z // 2, 2), AXES)
    placed = (P(AXES, None), P(AXES, None), P(AXES), P(), P())
    return jax.shard_map(
        body,
        mesh=cut,
        in_specs=placed,
        out_specs=(P(AXES, None), P(AXES, None)),
        check_vma=False,
    )
```

```python
import jax
import jax.numpy as jnp
from jax import lax
from jax.experimental import pallas as pl
from jax.experimental.pallas import tpu as pltpu
from jax.sharding import Mesh, PartitionSpec as P

STEPS = 2
GRP, Y_HI, Z = 16, 2, 32
AXES = ("grp", "y_hi", "z_hi", "z_lo")
REGION = ("grp", "y_hi", "z_lo")


def device_at(x, y, core, z):
    return (((x * 2 + y % 2) * 2 + core) * Y_HI + y // 2) * Z + z


def routes():
    in_plane, along_z = [], []
    for g in range(GRP):
        for y_hi in range(Y_HI):
            for z in range(Z):
                column = (3 * g + z + 8 * y_hi) % GRP
                z_lo = (2 * g - z) % Z // GRP
                source = (g * Y_HI + y_hi) * Z + z
                via = device_at(column // 4, column % 4, y_hi, z)
                held = device_at(column // 4, column % 4, y_hi, 2 * g + z_lo)
                in_plane.append((source, via))
                along_z.append((via, held))
    return in_plane, along_z


IN_PLANE, ALONG_Z = routes()
VIA_TO_HELD = dict(ALONG_Z)
TO_REGION = [(source, VIA_TO_HELD[via]) for source, via in IN_PLANE]
FROM_REGION = [(held, source) for source, held in TO_REGION]


def owner_place(position):
    core, chip = position & 1, position >> 1
    x = (chip >> 2) & 3
    y = (chip - x) & 3
    return x, y, core, chip >> 4


def owner_device(owner):
    group, position = owner // 64, owner % 64
    x, y, core, z_lo = owner_place(position)
    return device_at(x, y, core, 2 * group + z_lo)


OWNERS = [owner_device(owner) for owner in range(GRP * Y_HI * Z)]
NEXT = [(OWNERS[i], OWNERS[(i + 1) % len(OWNERS)]) for i in range(len(OWNERS))]
BEFORE = [(b, a) for a, b in NEXT]


def moved(x, route):
    return lax.ppermute(x, AXES, route)


TILE = 384


def gradients_kernel(scale_ref, offset_ref, p0, p1, p2, c0, c1, c2, out_ref):
    slots, width = p0.shape
    scale, offset = scale_ref[0], offset_ref[0]
    shape = (slots, slots)
    same = lax.broadcasted_iota(jnp.int32, shape, 0) == lax.broadcasted_iota(jnp.int32, shape, 1)
    identity_square = jnp.where(same, jnp.float32(1.0), jnp.float32(0.0))

    def weights(left, right, matching_label):
        scores = lax.dot_general(
            left[...], right[...], (((1,), (1,)), ((), ())), preferred_element_type=jnp.float32
        )
        coef = jax.nn.sigmoid(scale * scores + offset) - matching_label
        return (scale * coef).astype(jnp.bfloat16)

    zero = jnp.float32(0.0)
    for rows, others, start in ((p0, (c0, c1, c2), 0), (c0, (p0, p1, p2), width)):
        mixed = [
            weights(rows, other, identity_square if n == 0 else zero)
            for n, other in enumerate(others)
        ]
        for at in range(0, width, TILE):
            total = sum(
                jnp.dot(w, other[:, at : at + TILE], preferred_element_type=jnp.float32)
                for w, other in zip(mixed, others)
            )
            out_ref[:, start + at : start + at + TILE] = total.astype(out_ref.dtype)


def gradients(scale, offset, pictures, captions):
    slots, width = pictures[0].shape
    arrays = [*pictures, *captions]
    flops = 12 * 2 * slots * slots * width
    return pl.pallas_call(
        gradients_kernel,
        out_shape=jax.ShapeDtypeStruct((slots, 2 * width), jnp.bfloat16),
        in_specs=[pl.BlockSpec(memory_space=pltpu.SMEM)] * 2
        + [pl.BlockSpec(memory_space=pltpu.VMEM)] * len(arrays),
        out_specs=pl.BlockSpec(memory_space=pltpu.VMEM),
        compiler_params=pltpu.CompilerParams(vmem_limit_bytes=24 * 1024 * 1024),
        cost_estimate=pl.CostEstimate(
            flops=flops, bytes_accessed=16 * slots * width, transcendentals=6 * slots * slots
        ),
        name="gradients",
    )(scale, offset, *arrays)


def times_rows(weights, rows):
    return jnp.dot(weights, rows, preferred_element_type=jnp.float32)


def rows_of_transpose(weights, rows):
    return lax.dot_general(
        weights, rows, (((0,), (0,)), ((), ())), preferred_element_type=jnp.float32
    )


def swap_blocks(x, devices):
    slots, width = x.shape
    out = lax.all_to_all(
        x.reshape(devices, slots // devices, width),
        REGION,
        split_axis=0,
        concat_axis=0,
        tiled=True,
    )
    return out.reshape(slots, width)


def body(picture_embeds, caption_embeds, holder_position, score_scaling, score_offset_term):
    rows_here, width = picture_embeds.shape
    devices = lax.axis_size(REGION)
    capacity = 2 * rows_here // devices
    slots = devices * capacity

    position = moved(holder_position, TO_REGION)
    both = jnp.concatenate([picture_embeds, caption_embeds], axis=1)
    held = moved(moved(both, IN_PLANE), ALONG_Z)

    same = position[:, None] == position[None, :]
    order = jnp.arange(rows_here, dtype=jnp.int32)
    rank_in = jnp.sum((same & (order[None, :] < order[:, None])).astype(jnp.int32), axis=1)
    x, y, core, z_lo = owner_place(position)
    owner = (((x * 2 + (y & 1)) * 2 + core) * 2 + (y >> 1)) * 2 + z_lo
    placer = (
        jnp.arange(slots, dtype=jnp.int32)[:, None] == (owner * capacity + rank_in)[None, :]
    ).astype(jnp.bfloat16)

    received = swap_blocks(times_rows(placer, held).astype(jnp.bfloat16), devices)
    pictures = received[:, :width]
    captions = received[:, width:]

    earlier_captions = [captions]
    later_pictures = [pictures]
    for _ in range(STEPS):
        earlier_captions.append(moved(earlier_captions[-1], NEXT))
        later_pictures.append(moved(later_pictures[-1], BEFORE))

    done = gradients(score_scaling, score_offset_term, later_pictures, earlier_captions)
    back = swap_blocks(done, devices)
    grads = rows_of_transpose(placer, back).astype(jnp.bfloat16)
    image_grad = moved(grads[:, :width], FROM_REGION)
    text_grad = moved(grads[:, width:], FROM_REGION)
    return (image_grad, text_grad)


def solution(mesh):
    cut = Mesh(mesh.devices.reshape(GRP, Y_HI, Z // 2, 2), AXES)
    placed = (P(AXES, None), P(AXES, None), P(AXES), P(), P())
    return jax.shard_map(
        body,
        mesh=cut,
        in_specs=placed,
        out_specs=(P(AXES, None), P(AXES, None)),
        check_vma=False,
    )
```
